256 devices in a mesh: rows: 16 (over z_hi, y), cols: 16 (over z_lo, x, core).
Axes of the slice: x: 4, y: 4, z: 8 (z_hi: 4, z_lo: 2; z = z_hi * 2 + z_lo), core: 2. Of those that a mesh axis runs over, the one named last changes fastest.
Arguments:
- features: bfloat16 [65536, 256], P(('cols', 'rows')), may hold values from -6 to 6
- weight: bfloat16 [256, 256], replicated, may hold values from -0.375 to 0.375
- tile_values: bfloat16 [16, 16, 768, 4096], P('rows', 'cols'), may hold values from -0.0546875 to 0.0546875
- tile_rows: int32 [16, 16, 768], P('rows', 'cols'), may hold values from 0 to 63
- tile_cols: int32 [16, 16, 768], P('rows', 'cols'), may hold values from 0 to 63
- tile_count: int32 [16, 16], P('rows', 'cols'), may hold values from 1 to 768, as said below
- out_grad: bfloat16 [65536, 256], P(('rows', 'cols')), may hold values from -6 to 6
Outputs:
- hidden: bfloat16 [65536, 256], P(('rows', 'cols'))
- feature_grad: bfloat16 [65536, 256], P(('cols', 'rows'))
- weight_grad: float32 [256, 256], P('rows', 'cols')
The draws below stay inside these ranges and needn't reach their ends.
Inputs may be any that keep to these rules, and one draw needn't show every extreme that they name: Device (r, c) holds tile_count[r, c] live tiles in its first slots; tiles may share a position and then add. Some device holds 768 live tiles in every draw.
All inputs are finite; a program needn't handle non-finite values.
Results may differ from the reference program's by a relative error of at most 0.007.
Values may be sent and summed in bfloat16 or wider, within the bound.
No kernel may reach another device: no remote copies, remote signals or barrier semaphores. Data moves between devices by JAX's collectives and lax.ppermute only.
A program may use at most 128 MiB of HBM per device.

```python
import jax
import jax.numpy as jnp
from jax import lax

F = 256
TB = 64
NODE_DEV = 256
TILES_DEV = 768
NODES = 65536
N_ROWS = 16
N_COLS = 16


def draw_tile_count(key, part):
    key = jax.random.fold_in(key, 7)
    key_light, key_heavy, key_pos = jax.random.split(key, 3)
    light = jax.random.randint(key_light, (N_ROWS, N_COLS), TILES_DEV // 8, TILES_DEV // 2 + 1)
    heavy = jax.random.randint(key_heavy, (N_ROWS, N_COLS), TILES_DEV // 2, TILES_DEV + 1)
    dst_group = NODE_DEV * N_COLS
    src_group = NODE_DEV * N_ROWS
    row_ids = jnp.arange(N_ROWS, dtype=jnp.int32)[:, None]
    col_ids = jnp.arange(N_COLS, dtype=jnp.int32)[None, :]
    near = (row_ids * dst_group < (col_ids + 1) * src_group) & (col_ids * src_group < (row_ids + 1) * dst_group)
    counts = jnp.where(near, heavy, light).reshape(-1)
    position = jax.random.randint(key_pos, (), 0, N_ROWS * N_COLS)
    counts = counts.at[position].set(TILES_DEV)
    return counts.reshape(N_ROWS, N_COLS).astype(jnp.int32)


def with_ends(entries, stream_key, smallest, high):
    longest = entries.shape.index(max(entries.shape))
    spots = []
    for shift in (0, 1):
        where = [jax.random.randint(jax.random.fold_in(stream_key, axis), (), 0, length) for axis, length in enumerate(entries.shape)]
        where[longest] = (where[longest] + shift) % entries.shape[longest]
        spots.append(tuple(where))
    return entries.at[spots[0]].set(smallest).at[spots[1]].set(high)


def steps_of(key, extent, pieces, smallest, high):
    level, own = 1.0, jax.random.fold_in(key, 6)
    for axis_at, blocks in pieces:
        steps = jnp.exp(jax.random.uniform(jax.random.fold_in(own, axis_at), (blocks,), jnp.float32, smallest / len(pieces), high / len(pieces)))
        level = level * jnp.repeat(steps, extent[axis_at] // blocks).reshape([-1 if axis == axis_at else 1 for axis in range(len(extent))])
    return level


def centred(stream_key, extent, width, most, cuts=(), kind=jnp.bfloat16):
    level = steps_of(stream_key, extent, cuts, -0.22, 0.18) if cuts else 1.0
    drawn = jax.random.normal(stream_key, extent, jnp.float32) * width * level
    return jnp.minimum(jnp.maximum(drawn, -most), most).astype(kind)


def setup_inputs(seed: int = 0) -> dict:
    key_of = jax.random.split(jax.random.key(seed), 8)
    features = centred(key_of[0], (NODES, F), 1.0, 6.0, ((0, 256),))
    weight = centred(key_of[1], (F, F), F ** -0.5, 0.375)
    tile_values = centred(key_of[2], (N_ROWS, N_COLS, TILES_DEV, TB * TB), (TB * TB * TILES_DEV // NODE_DEV) ** -0.5, 0.0546875, ((0, 16), (1, 16)))
    tile_rows = with_ends(jax.random.randint(key_of[3], (N_ROWS, N_COLS, TILES_DEV), 0, NODE_DEV * N_COLS // TB), jax.random.fold_in(key_of[3], 1), 0, (NODE_DEV * N_COLS // TB) - 1).astype(jnp.int32)
    tile_cols = with_ends(jax.random.randint(key_of[4], (N_ROWS, N_COLS, TILES_DEV), 0, NODE_DEV * N_ROWS // TB), jax.random.fold_in(key_of[4], 1), 0, (NODE_DEV * N_ROWS // TB) - 1).astype(jnp.int32)
    tile_count = draw_tile_count(jax.random.fold_in(key_of[7], 71), 0)
    out_grad = centred(key_of[6], (NODES, F), 1.0, 6.0, ((0, 256),))
    return dict(features=features, weight=weight, tile_values=tile_values, tile_rows=tile_rows, tile_cols=tile_cols, tile_count=tile_count, out_grad=out_grad)


def reference(features, weight, tile_values, tile_rows, tile_cols, tile_count, out_grad):
    dst_group = NODE_DEV * N_COLS
    src_group = NODE_DEV * N_ROWS
    nodes = NODE_DEV * N_ROWS * N_COLS
    nblocks = nodes // TB
    devices = N_ROWS * N_COLS
    projected = jnp.dot(features, weight, preferred_element_type=jnp.float32).astype(jnp.bfloat16)
    live = (jnp.arange(TILES_DEV, dtype=jnp.int32)[None, None, :] < tile_count[:, :, None])
    grow = (jnp.arange(N_ROWS, dtype=jnp.int32)[:, None, None] * (dst_group // TB) + tile_rows).astype(jnp.int32)
    gcol = (jnp.arange(N_COLS, dtype=jnp.int32)[None, :, None] * (src_group // TB) + tile_cols).astype(jnp.int32)
    grow = grow.reshape(devices, TILES_DEV)
    gcol = gcol.reshape(devices, TILES_DEV)
    livef = live.reshape(devices, TILES_DEV)
    vals = tile_values.reshape(devices, TILES_DEV, TB, TB)
    proj3 = projected.reshape(nblocks, TB, F)

    def forward(acc, index):
        values = vals[index].astype(jnp.float32)
        source = proj3[gcol[index]].astype(jnp.float32)
        prod = jnp.einsum("kij,kjf->kif", values, source)
        prod = jnp.where(livef[index][:, None, None], prod, jnp.float32(0.0))
        return acc.at[grow[index]].add(prod), None

    acc, unused = lax.scan(forward, jnp.zeros((nblocks, TB, F), jnp.float32), jnp.arange(devices, dtype=jnp.int32))
    summed = acc.reshape(nodes, F)
    sig = jax.nn.sigmoid(summed)
    hidden = (summed * sig).astype(jnp.bfloat16)
    slope = (out_grad.astype(jnp.float32) * sig * (1.0 + summed * (1.0 - sig))).astype(jnp.bfloat16)
    slope3 = slope.reshape(nblocks, TB, F)

    def backward(acc, index):
        values = vals[index].astype(jnp.float32)
        source = slope3[grow[index]].astype(jnp.float32)
        prod = jnp.einsum("kij,kif->kjf", values, source)
        prod = jnp.where(livef[index][:, None, None], prod, jnp.float32(0.0))
        return acc.at[gcol[index]].add(prod), None

    acc2, unused2 = lax.scan(backward, jnp.zeros((nblocks, TB, F), jnp.float32), jnp.arange(devices, dtype=jnp.int32))
    back = acc2.reshape(nodes, F).astype(jnp.bfloat16)
    feature_grad = jnp.dot(back, weight.T, preferred_element_type=jnp.float32).astype(jnp.bfloat16)
    weight_grad = jnp.dot(features.T, back, preferred_element_type=jnp.float32)
    return hidden, feature_grad, weight_grad
```

```python
import functools
import jax
import jax.numpy as jnp
from jax import lax
from jax.experimental import pallas as pl
from jax.experimental.pallas import tpu as pltpu
from jax.sharding import PartitionSpec as P

TB = 64
GROUP = 16
PAIRS = TB // 2


def build_kernel(blocks, tiles, slab, count_ref, rows_ref, cols_ref, vals_ref, out_ref,
                 dense, sums, lay, slot_of, place_of, used, sem):
    turn = pl.program_id(0)
    count = count_ref[0]
    spare = blocks * blocks

    @pl.when(turn == 0)
    def _():
        def clear(i, carry):
            dense[pl.ds(pl.multiple_of(i * TB, TB), TB), :] = jnp.zeros((TB, dense.shape[1]), dense.dtype)
            for j in range(blocks):
                slot_of[i * blocks + j] = -1
            return carry
        lax.fori_loop(0, blocks, clear, 0)

        def unplace(i, carry):
            for j in range(GROUP):
                place_of[i * GROUP + j] = spare
            return carry
        lax.fori_loop(0, tiles // GROUP, unplace, 0)
        slot_of[spare] = tiles
        used[0] = 0

    def gather(g, carry):
        base = turn * slab + g * GROUP

        @pl.when(base < count)
        def _():
            for m in range(PAIRS):
                lay[m * GROUP:(m + 1) * GROUP, :] = vals_ref[
                    pl.ds(pl.multiple_of(g * GROUP, GROUP), GROUP), m * 128:(m + 1) * 128
                ].astype(jnp.float32)
            top = used[0]
            for k in range(GROUP):
                index = base + k
                place = jnp.where(index < count, rows_ref[index] * blocks + cols_ref[index], spare)
                slot = slot_of[place]
                fresh = slot < 0
                slot = jnp.where(fresh, top, slot)
                slot_of[place] = slot

                @pl.when(fresh)
                def _():
                    place_of[slot] = place
                top = jnp.where(fresh, top + 1, top)
                tile = lay[pl.ds(k, PAIRS, stride=GROUP), :]
                sums[slot] = tile + jnp.where(fresh, 0.0, sums[slot])
            used[0] = top
        return carry

    lax.fori_loop(0, slab // GROUP, gather, 0)

    @pl.when(turn == pl.num_programs(0) - 1)
    def _():
        lane_half = lax.broadcasted_iota(jnp.int32, (PAIRS, 128), 1) // TB

        def put(i, carry):
            for k in range(8):
                slot = i * 8 + k
                place = place_of[slot]
                row = place // blocks
                col = place % blocks
                half = col % 2
                tile = sums[slot]
                turned = pltpu.roll(tile, TB, 1)
                even = half == 0
                mine = lane_half == half
                lanes = pl.ds(pl.multiple_of((col // 2) * 128, 128), 128)
                for odd in range(2):
                    here = (pl.ds(pl.multiple_of(row * TB + odd * PAIRS, PAIRS), PAIRS), lanes)
                    if odd:
                        new = jnp.where(even, turned, tile)
                    else:
                        new = jnp.where(even, tile, turned)
                    old = dense[here].astype(jnp.float32)
                    dense[here] = jnp.where(mine, new, old).astype(dense.dtype)
            return carry

        lax.fori_loop(0, (used[0] + 7) // 8, put, 0)
        copy = pltpu.make_async_copy(dense.at[pl.ds(0, blocks * TB)], out_ref, sem)
        copy.start()
        copy.wait()


def build_dense(values, rows, cols, count, blocks, slab=128):
    tiles = values.shape[0]
    n = blocks * TB
    return pl.pallas_call(
        functools.partial(build_kernel, blocks, tiles, slab),
        grid=(tiles // slab,),
        in_specs=[
            pl.BlockSpec(memory_space=pltpu.SMEM),
            pl.BlockSpec(memory_space=pltpu.SMEM),
            pl.BlockSpec(memory_space=pltpu.SMEM),
            pl.BlockSpec((slab, TB * TB), lambda i: (i, 0)),
        ],
        out_specs=pl.BlockSpec(memory_space=pl.ANY),
        out_shape=jax.ShapeDtypeStruct((n, n), jnp.bfloat16),
        scratch_shapes=[
            pltpu.VMEM((n + TB, n), jnp.bfloat16),
            pltpu.VMEM((tiles + 1, PAIRS, 128), jnp.float32),
            pltpu.VMEM((GROUP * PAIRS, 128), jnp.float32),
            pltpu.SMEM((blocks * blocks + 1,), jnp.int32),
            pltpu.SMEM((tiles,), jnp.int32),
            pltpu.SMEM((1,), jnp.int32),
            pltpu.SemaphoreType.DMA,
        ],
        compiler_params=pltpu.CompilerParams(vmem_limit_bytes=56 * 1024 * 1024),
        cost_estimate=pl.CostEstimate(flops=0, bytes_accessed=64 * 1024 * 1024, transcendentals=0),
        name="build_dense",
    )(count, rows, cols, values)


def rows_shift(dz, dy):
    return [(z * 4 + y, (z + dz) % 4 * 4 + (y + dy) % 4) for z in range(4) for y in range(4)]


def cols_shift(dz, dx, dc):
    return [
        (z * 8 + x * 2 + c, (z + dz) % 2 * 8 + (x + dx) % 4 * 2 + (c + dc) % 2)
        for z in range(2) for x in range(4) for c in range(2)
    ]


def f32(x):
    return x.astype(jnp.float32)


def bf16(x):
    return x.astype(jnp.bfloat16)


def mix():
    nodes = lax.broadcasted_iota(jnp.int32, (256, 256), 0)
    natural = lax.broadcasted_iota(jnp.int32, (256, 256), 1)
    inner = nodes % TB
    source = nodes // TB * TB + inner % PAIRS * 2 + inner // PAIRS
    return bf16(source == natural)


def body(features, weight, tile_values, tile_rows, tile_cols, tile_count, out_grad):
    me_r = lax.axis_index("rows")
    me_c = lax.axis_index("cols")
    own = tile_rows[0, 0] // 4
    slot_r = (own % 2 - me_c % 2) % 2 * 8 + (own // 2 % 4 - me_c // 2 % 4) % 4 * 2 + (own // 8 - me_c // 8) % 2
    rows = slot_r * 4 + tile_rows[0, 0] % 4
    own = tile_cols[0, 0] // 4
    slot_c = (own % 4 - me_r % 4) % 4 * 4 + (own // 4 - me_r // 4) % 4
    cols = slot_c * 4 + tile_cols[0, 0] % 4

    with jax.named_scope("gather_features"):
        block = jnp.concatenate(
            [features]
            + [lax.ppermute(features, "rows", rows_shift(-dz, 0)) for dz in (1, 2, 3)], 0)
        sources = jnp.concatenate(
            [block] + [lax.ppermute(block, "rows", rows_shift(0, -dy)) for dy in (1, 2, 3)], 0)
    with jax.named_scope("build"):
        dense = build_dense(tile_values[0, 0], rows, cols, tile_count[0], 64)
    with jax.named_scope("project"):
        projected = bf16(jnp.dot(sources, weight, preferred_element_type=jnp.float32))
    with jax.named_scope("forward"):
        messages = bf16(jnp.dot(dense, projected, preferred_element_type=jnp.float32))
    with jax.named_scope("reduce_cols"):
        got = lax.ppermute(messages[2048:], "cols", cols_shift(0, 0, 1))
        part = f32(messages[:2048]) + f32(got)
        sent = bf16(part[512:])
        got = [lax.ppermute(sent[512 * (d - 1):512 * d], "cols", cols_shift(0, d, 0)) for d in (1, 2, 3)]
        part = part[:512] + f32(got[0]) + f32(got[1]) + f32(got[2])
        got = lax.ppermute(bf16(part[256:]), "cols", cols_shift(1, 0, 0))
        summed = part[:256] + f32(got)
    with jax.named_scope("activate"):
        order = mix()
        grad = jnp.dot(order, out_grad, preferred_element_type=jnp.float32)
        sig = jax.nn.sigmoid(summed)
        hidden = bf16(summed * sig)
        slope = bf16(grad * sig * (1.0 + summed * (1.0 - sig)))
        hidden = bf16(lax.dot_general(order, hidden, (((0,), (0,)), ((), ())), preferred_element_type=jnp.float32))
    with jax.named_scope("gather_slope"):
        block = jnp.concatenate([slope, lax.ppermute(slope, "cols", cols_shift(1, 0, 0))], 0)
        block = jnp.concatenate(
            [block] + [lax.ppermute(block, "cols", cols_shift(0, -d, 0)) for d in (1, 2, 3)], 0)
        slopes = jnp.concatenate([block, lax.ppermute(block, "cols", cols_shift(0, 0, 1))], 0)
    with jax.named_scope("backward"):
        terms = bf16(lax.dot_general(dense, slopes, (((0,), (0,)), ((), ())), preferred_element_type=jnp.float32))
    with jax.named_scope("reduce_rows"):
        got = [lax.ppermute(terms[1024 * d:1024 * (d + 1)], "rows", rows_shift(0, d)) for d in (1, 2, 3)]
        part = f32(terms[:1024]) + f32(got[0]) + f32(got[1]) + f32(got[2])
        sent = bf16(part[256:])
        got = [lax.ppermute(sent[256 * (d - 1):256 * d], "rows", rows_shift(d, 0)) for d in (1, 2, 3)]
        back = bf16(part[:256] + f32(got[0]) + f32(got[1]) + f32(got[2]))
    with jax.named_scope("feature_grad"):
        feature_grad = bf16(lax.dot_general(
            back, weight, (((1,), (1,)), ((), ())), preferred_element_type=jnp.float32))
    with jax.named_scope("weight_grad"):
        share = lax.dot_general(sources, terms, (((0,), (0,)), ((), ())), preferred_element_type=jnp.float32)
        band = lax.all_to_all(share, "rows", 0, 0, tiled=True)
        band = jnp.sum(band.reshape(16, 16, 256), axis=0)
        band = band.reshape(16, 16, 16).transpose(1, 0, 2).reshape(16, 256)
        band = lax.all_to_all(band, "cols", 0, 0, tiled=True)
        weight_grad = jnp.sum(band, axis=0).reshape(16, 16)
    return hidden, feature_grad, weight_grad


def solution(mesh):
    return jax.shard_map(
        body,
        mesh=mesh,
        in_specs=(
            P(("cols", "rows"), None),
            P(),
            P("rows", "cols", None, None),
            P("rows", "cols", None),
            P("rows", "cols", None),
            P("rows", "cols"),
            P(("rows", "cols"), None),
        ),
        out_specs=(P(("rows", "cols"), None), P(("cols", "rows"), None), P("rows", "cols")),
        check_vma=False,
    )
```

```python
import functools
import jax
import jax.numpy as jnp
from jax import lax
from jax.experimental import pallas as pl
from jax.experimental.pallas import tpu as pltpu
from jax.sharding import PartitionSpec as P

TB = 64
PAIRS = TB // 2
GROUP = 16
SIDE = 64
TILES = 768
BANDS = 8
BAND = SIDE * TB // BANDS
WIDE = SIDE // 2
F = 256
UNROLL = 8
NODES = SIDE * TB
VMEM_LIMIT = 56 * 1024 * 1024


def plan_tiles(rows, cols, count):
    index = jnp.arange(TILES, dtype=jnp.int32)
    live = index < count
    pair = rows * WIDE + (cols >> 1)
    key = jnp.where(live, pair, SIDE * WIDE) * 1024 + index
    rank = jnp.sum((key[None, :] < key[:, None]).astype(jnp.int32), axis=1)
    code = index + 1024 * (pair & (BAND // TB * WIDE - 1))
    order = jnp.sum(jnp.where(rank[None, :] == index[:, None], code[None, :], 0), axis=1)
    bands = jnp.arange(BANDS + 1, dtype=jnp.int32)
    edge = bands * (BAND // TB * WIDE * 1024)
    starts = jnp.sum((key[None, :] < edge[:, None]).astype(jnp.int32), axis=1)
    return order, starts


def build_kernel(slab, order_ref, starts_ref, cols_ref, vals_ref, after_ref, dense_ref, turned_ref, lay):
    turn = pl.program_id(0)
    slabs = TILES // slab

    @pl.when(turn < slabs)
    def _():
        lane_half = lax.broadcasted_iota(jnp.int32, (PAIRS, 128), 1) >> 6

        def relay(g, carry):
            for m in range(PAIRS):
                lay[m * GROUP:(m + 1) * GROUP, :] = vals_ref[
                    pl.ds(pl.multiple_of(g * GROUP, GROUP), GROUP), m * 128:(m + 1) * 128
                ].astype(jnp.float32)
            base = turn * slab + g * GROUP
            for k in range(GROUP):
                tile = lay[pl.ds(k, PAIRS, stride=GROUP), :]
                other = pltpu.roll(tile, TB, 1)
                right = cols_ref[base + k] & 1
                mine = lane_half == right
                left = right == 0
                turned_ref[base + k, :PAIRS] = jnp.where(
                    mine, jnp.where(left, tile, other), 0.0).astype(turned_ref.dtype)
                turned_ref[base + k, PAIRS:] = jnp.where(
                    mine, jnp.where(left, other, tile), 0.0).astype(turned_ref.dtype)
            return carry

        lax.fori_loop(0, slab // GROUP, relay, 0)

    @pl.when(turn >= slabs)
    def _():
        low = starts_ref[turn - slabs]
        high = starts_ref[turn - slabs + 1]
        dense_ref[...] = jnp.zeros(dense_ref.shape, dense_ref.dtype)

        def put(i, carry):
            before, block = carry
            for k in range(UNROLL):
                spot = low + i * UNROLL + k
                code = order_ref[jnp.minimum(spot, high - 1)]
                place = code >> 10
                keep = jnp.where(place == before, 1.0, 0.0)
                add = jnp.where(spot < high, 1.0, 0.0)
                block = block * keep + turned_ref[code & 1023].astype(jnp.float32) * add
                before = place
                rows = pl.ds(pl.multiple_of((place >> 5) << 6, TB), TB)
                lanes = pl.ds(pl.multiple_of((place & 31) << 7, 128), 128)
                dense_ref[rows, lanes] = block.astype(dense_ref.dtype)
            return before, block

        none = jnp.zeros((TB, 128), jnp.float32)
        lax.fori_loop(0, (high - low + UNROLL - 1) >> 3, put, (jnp.int32(-1), none))


def build_dense(values, cols, order, starts, after, slab=256):
    slabs = TILES // slab
    return pl.pallas_call(
        functools.partial(build_kernel, slab),
        grid=(slabs + BANDS,),
        in_specs=[
            pl.BlockSpec(memory_space=pltpu.SMEM),
            pl.BlockSpec(memory_space=pltpu.SMEM),
            pl.BlockSpec(memory_space=pltpu.SMEM),
            pl.BlockSpec((slab, TB * TB), lambda i: (jnp.minimum(i, slabs - 1), 0)),
            pl.BlockSpec(memory_space=pl.ANY),
        ],
        out_specs=pl.BlockSpec((BAND, NODES), lambda i: (jnp.maximum(i - slabs, 0), 0)),
        out_shape=jax.ShapeDtypeStruct((NODES, NODES), jnp.bfloat16),
        scratch_shapes=[
            pltpu.VMEM((TILES, TB, 128), jnp.bfloat16),
            pltpu.VMEM((GROUP * PAIRS, 128), jnp.float32),
        ],
        compiler_params=pltpu.CompilerParams(vmem_limit_bytes=VMEM_LIMIT),
        cost_estimate=pl.CostEstimate(flops=0, bytes_accessed=45 * 1024 * 1024, transcendentals=0),
        name="build_dense",
    )(order, starts, cols, values, after)


def forward_kernel(after_ref, dense_ref, *refs):
    pieces, (keep_ref, send_ref), whole = refs[:-3], refs[-3:-1], refs[-1]
    turn = pl.program_id(0)

    @pl.when(turn == 0)
    def _():
        for k, piece in enumerate(pieces):
            size = piece.shape[0]
            whole[k * size:(k + 1) * size, :] = piece[...]

    total = jnp.dot(dense_ref[...], whole[...], preferred_element_type=jnp.float32)

    @pl.when(turn == 0)
    def _():
        send_ref[...] = total.astype(send_ref.dtype)

    @pl.when(turn == 1)
    def _():
        keep_ref[...] = total.astype(keep_ref.dtype)


def forward_part(dense, pieces, dx, after):
    half = NODES // 8
    out = pl.BlockSpec((half, F), lambda i: (0, 0))
    return pl.pallas_call(
        forward_kernel,
        grid=(2,),
        in_specs=[pl.BlockSpec(memory_space=pl.ANY), pl.BlockSpec((half, NODES), lambda i: (2 * dx + 1 - i, 0))]
        + [pl.BlockSpec(p.shape, lambda i: (0, 0)) for p in pieces],
        out_specs=[out, out],
        out_shape=[jax.ShapeDtypeStruct((half, F), jnp.bfloat16)] * 2,
        scratch_shapes=[pltpu.VMEM((NODES, F), jnp.bfloat16)],
        compiler_params=pltpu.CompilerParams(vmem_limit_bytes=VMEM_LIMIT),
        cost_estimate=pl.CostEstimate(
            flops=4 * half * NODES * F, bytes_accessed=11 * 1024 * 1024, transcendentals=0),
        name="forward_part",
    )(after, dense, *pieces)


def backward_kernel(after_ref, dense_ref, *refs):
    pieces, out_ref, whole = refs[:-2], refs[-2], refs[-1]

    @pl.when(pl.program_id(0) == 0)
    def _():
        for k, piece in enumerate(pieces):
            size = piece.shape[0]
            whole[k * size:(k + 1) * size, :] = piece[...]

    out_ref[...] = lax.dot_general(
        dense_ref[...], whole[...], (((0,), (0,)), ((), ())), preferred_element_type=jnp.float32
    ).astype(out_ref.dtype)


def backward_part(dense, pieces, dy, after, width=512):
    part = NODES // 4
    steps = part // width
    return pl.pallas_call(
        backward_kernel,
        grid=(steps,),
        in_specs=[pl.BlockSpec(memory_space=pl.ANY), pl.BlockSpec((NODES, width), lambda i: (0, steps * dy + i))]
        + [pl.BlockSpec(p.shape, lambda i: (0, 0)) for p in pieces],
        out_specs=pl.BlockSpec((width, F), lambda i: (i, 0)),
        out_shape=jax.ShapeDtypeStruct((part, F), jnp.bfloat16),
        scratch_shapes=[pltpu.VMEM((NODES, F), jnp.bfloat16)],
        compiler_params=pltpu.CompilerParams(vmem_limit_bytes=VMEM_LIMIT),
        cost_estimate=pl.CostEstimate(
            flops=2 * part * NODES * F, bytes_accessed=11 * 1024 * 1024, transcendentals=0),
        name="backward_part",
    )(after, dense, *pieces)


def rows_shift(dz, dy):
    return [(z * 4 + y, (z + dz) % 4 * 4 + (y + dy) % 4) for z in range(4) for y in range(4)]


def cols_shift(dz, dx, dc):
    return [
        (z * 8 + x * 2 + c, (z + dz) % 2 * 8 + (x + dx) % 4 * 2 + (c + dc) % 2)
        for z in range(2) for x in range(4) for c in range(2)
    ]


def f32(x):
    return x.astype(jnp.float32)


def bf16(x):
    return x.astype(jnp.bfloat16)


def dot(a, b, ca=1, cb=0):
    return lax.dot_general(a, b, (((ca,), (cb,)), ((), ())), preferred_element_type=jnp.float32)


def mix():
    nodes = lax.broadcasted_iota(jnp.int32, (256, 256), 0)
    natural = lax.broadcasted_iota(jnp.int32, (256, 256), 1)
    inner = nodes & (TB - 1)
    source = (nodes & ~(TB - 1)) + (inner & (PAIRS - 1)) * 2 + (inner >> 5)
    return bf16(source == natural)


def body(features, weight, tile_values, tile_rows, tile_cols, tile_count, out_grad):
    me_r = lax.axis_index("rows")
    me_c = lax.axis_index("cols")
    own = tile_rows[0, 0] >> 2
    slot_r = (((own >> 1) - (me_c >> 1)) & 3) * 4 + ((own ^ me_c) & 1) * 2 + (((own ^ me_c) >> 3) & 1)
    rows = slot_r * 4 + (tile_rows[0, 0] & 3)
    own = tile_cols[0, 0] >> 2
    slot_c = ((own - me_r) & 3) * 4 + (((own >> 2) - (me_r >> 2)) & 3)
    cols = slot_c * 4 + (tile_cols[0, 0] & 3)

    with jax.named_scope("gather_features"):
        block = jnp.concatenate(
            [features] + [lax.ppermute(features, "rows", rows_shift(-dz, 0)) for dz in (1, 2, 3)], 0)
        sources = [block] + [lax.ppermute(block, "rows", rows_shift(0, -dy)) for dy in (1, 2, 3)]
    with jax.named_scope("build"):
        order, starts = plan_tiles(rows, cols, tile_count[0, 0])
        dense = build_dense(tile_values[0, 0], cols, order, starts, block)
    parts = {}
    after = block
    for dx in (2, 1, 3, 0):
        with jax.named_scope("forward"):
            keep, send = forward_part(dense, sources, dx, after)
        with jax.named_scope("reduce_cols"):
            after = parts.get("sent", block)
            part = f32(keep) + f32(lax.ppermute(send, "cols", cols_shift(0, 0, 1)))
            if dx:
                parts["sent"] = bf16(part)
                part = f32(lax.ppermute(parts["sent"], "cols", cols_shift(0, dx, 0)))
            parts[dx] = part
    with jax.named_scope("reduce_cols"):
        part = parts[0] + parts[1] + parts[2] + parts[3]
        got = lax.ppermute(bf16(part[256:]), "cols", cols_shift(1, 0, 0))
        gathered = part[:256] + f32(got)
        high = bf16(gathered)
        low = bf16(gathered - f32(high))
        summed = dot(high, weight) + dot(low, weight)
    with jax.named_scope("activate"):
        order = mix()
        grad = dot(order, out_grad)
        sig = jax.nn.sigmoid(summed)
        slope = bf16(grad * sig * (1.0 + summed * (1.0 - sig)))
        hidden = bf16(dot(order, bf16(summed * sig), 0, 0))
    with jax.named_scope("gather_slope"):
        block = jnp.concatenate([slope, lax.ppermute(slope, "cols", cols_shift(1, 0, 0))], 0)
        slopes = []
        for dx in range(4):
            mine = lax.ppermute(block, "cols", cols_shift(0, -dx, 0)) if dx else block
            slopes += [mine, lax.ppermute(mine, "cols", cols_shift(0, 0, 1))]
    with jax.named_scope("weight_grad"):
        share = dot(high, slope, 0, 0) + dot(low, slope, 0, 0)
        band = lax.all_to_all(share, "rows", 0, 0, tiled=True)
    terms, got = {}, {}
    for dy in (2, 1, 3, 0):
        with jax.named_scope("backward"):
            terms[dy] = backward_part(dense, slopes, dy, band)
        with jax.named_scope("reduce_rows"):
            got[dy] = lax.ppermute(terms[dy], "rows", rows_shift(0, dy)) if dy else terms[dy]
    with jax.named_scope("reduce_rows"):
        part = f32(got[0]) + f32(got[1]) + f32(got[2]) + f32(got[3])
        sent = bf16(part[256:])
        got = [lax.ppermute(sent[256 * (d - 1):256 * d], "rows", rows_shift(d, 0)) for d in (1, 2, 3)]
        back = bf16(part[:256] + f32(got[0]) + f32(got[1]) + f32(got[2]))
    with jax.named_scope("feature_grad"):
        feature_grad = bf16(dot(back, weight, 1, 1))
    with jax.named_scope("weight_grad"):
        band = jnp.sum(band.reshape(16, 16, 256), axis=0)
        band = band.reshape(16, 16, 16).transpose(1, 0, 2).reshape(16, 256)
        band = lax.all_to_all(band, "cols", 0, 0, tiled=True)
        weight_grad = jnp.sum(band, axis=0).reshape(16, 16)
    return hidden, feature_grad, weight_grad


def solution(mesh):
    return jax.shard_map(
        body,
        mesh=mesh,
        in_specs=(
            P(("cols", "rows"), None),
            P(),
            P("rows", "cols", None, None),
            P("rows", "cols", None),
            P("rows", "cols", None),
            P("rows", "cols"),
            P(("rows", "cols"), None),
        ),
        out_specs=(P(("rows", "cols"), None), P(("cols", "rows"), None), P("rows", "cols")),
        check_vma=False,
    )
```

```python
import functools
import jax
import jax.numpy as jnp
from jax import lax
from jax.experimental import pallas as pl
from jax.experimental.pallas import tpu as pltpu
from jax.sharding import PartitionSpec as P

TB = 64
PAIRS = TB // 2
GROUP = 16
SIDE = 64
TILES = 768
WIDE = SIDE // 2
F = 256
PARTS = 4
UNROLL = 8
NODES = SIDE * TB
SLAB = 64


def plan_tiles(rows, cols, count):
    index = jnp.arange(TILES, dtype=jnp.int32)
    live = index < count
    pair = rows * WIDE + (cols >> 1)
    key = jnp.where(live, pair, SIDE * WIDE) * 1024 + index
    rank = jnp.sum((key[None, :] < key[:, None]).astype(jnp.int32), axis=1)
    code = index + 1024 * pair
    order = jnp.sum(jnp.where(rank[None, :] == index[:, None], code[None, :], 0), axis=1)
    edges = (jnp.arange(PARTS, dtype=jnp.int32) + 1) * (SIDE // PARTS)
    ends = jnp.sum((live[None, :] & (rows[None, :] < edges[:, None])).astype(jnp.int32), axis=1)
    return order, ends


def build_kernel(order_ref, ends_ref, cols_ref, vals_ref, after_ref, *refs):
    out_ref, *parts = refs[:PARTS]
    staged, vals, turned_ref, lay, sems = refs[PARTS:]
    parts = [staged, *parts]
    slabs = TILES // SLAB
    lane_half = lax.broadcasted_iota(jnp.int32, (PAIRS, 128), 1) >> 6

    def fetch(i):
        return pltpu.make_async_copy(vals_ref.at[pl.ds(i * SLAB, SLAB)], vals.at[i & 1], sems.at[i & 1])

    fetch(0).start()

    def clear(i, carry):
        rows = pl.ds(pl.multiple_of(i * (TB // PARTS), TB // PARTS), TB // PARTS)
        for dense_ref in parts:
            dense_ref[rows, :] = jnp.zeros((TB // PARTS, NODES), dense_ref.dtype)
        return carry

    def relay_slab(i, carry):
        @pl.when(i + 1 < slabs)
        def _():
            fetch(i + 1).start()

        lax.fori_loop(i * (SIDE // slabs), (i + 1) * (SIDE // slabs), clear, 0)
        fetch(i).wait()

        def relay(g, carry):
            for m in range(PAIRS):
                lay[m * GROUP:(m + 1) * GROUP, :] = vals[
                    i & 1, pl.ds(pl.multiple_of(g * GROUP, GROUP), GROUP), m * 128:(m + 1) * 128
                ].astype(jnp.float32)
            base = i * SLAB + g * GROUP
            for k in range(GROUP):
                turned_ref[base + k] = lay[pl.ds(k, PAIRS, stride=GROUP), :].astype(turned_ref.dtype)
            return carry

        lax.fori_loop(0, SLAB // GROUP, relay, 0)
        return carry

    lax.fori_loop(0, slabs, relay_slab, 0)
    lax.fori_loop(slabs * (SIDE // slabs), SIDE, clear, 0)
    none = jnp.zeros((PAIRS, 128), jnp.float32)
    for part, dense_ref in enumerate(parts):
        begin = ends_ref[part - 1] if part else 0
        end = ends_ref[part]

        def put(i, carry):
            before, even, odd = carry
            for k in range(UNROLL):
                spot = begin + i * UNROLL + k
                code = order_ref[jnp.minimum(spot, end - 1)]
                place = (code >> 10) & (SIDE // PARTS * WIDE - 1)
                keep = jnp.where(place == before, 1.0, 0.0)
                right = cols_ref[code & 1023] & 1
                tile = turned_ref[code & 1023].astype(jnp.float32)
                other = pltpu.roll(tile, TB, 1)
                mine = lane_half == jnp.where(spot < end, right, 2)
                left = right == 0
                even = even * keep + jnp.where(mine, jnp.where(left, tile, other), 0.0)
                odd = odd * keep + jnp.where(mine, jnp.where(left, other, tile), 0.0)
                before = place
                top = pl.multiple_of((place >> 5) << 6, TB)
                lanes = pl.ds(pl.multiple_of((place & 31) << 7, 128), 128)
                dense_ref[pl.ds(top, PAIRS), lanes] = even.astype(dense_ref.dtype)
                dense_ref[pl.ds(top + PAIRS, PAIRS), lanes] = odd.astype(dense_ref.dtype)
            return before, even, odd

        lax.fori_loop(0, (end - begin + UNROLL - 1) >> 3, put, (jnp.int32(-1), none, none))
        if part == 0:
            store = pltpu.make_async_copy(staged, out_ref, sems.at[2])
            store.start()
    store.wait()


def build_dense(values, cols, order, ends, after):
    smem = pl.BlockSpec(memory_space=pltpu.SMEM)
    anywhere = pl.BlockSpec(memory_space=pl.ANY)
    return pl.pallas_call(
        build_kernel,
        in_specs=[smem, smem, smem, pl.BlockSpec(memory_space=pltpu.HBM), anywhere],
        out_specs=[pl.BlockSpec(memory_space=pltpu.HBM)] + [pl.BlockSpec(memory_space=pltpu.VMEM)] * (PARTS - 1),
        out_shape=[pltpu.HBM((NODES // PARTS, NODES), jnp.bfloat16)]
        + [pltpu.VMEM((NODES // PARTS, NODES), jnp.bfloat16)] * (PARTS - 1),
        scratch_shapes=[
            pltpu.VMEM((NODES // PARTS, NODES), jnp.bfloat16),
            pltpu.VMEM((2, SLAB, TB * TB), jnp.bfloat16),
            pltpu.VMEM((TILES, PAIRS, 128), jnp.bfloat16),
            pltpu.VMEM((GROUP * PAIRS, 128), jnp.float32),
            pltpu.SemaphoreType.DMA((3,)),
        ],
        compiler_params=pltpu.CompilerParams(vmem_limit_bytes=17 * 1024 * 1024),
        cost_estimate=pl.CostEstimate(flops=0, bytes_accessed=0, transcendentals=0),
        name="build_dense",
    )(order, ends, cols, pltpu.with_memory_space_constraint(values, pltpu.HBM), after)


def forward_kernel(after_ref, *refs):
    bands, pieces, (keep_ref, send_ref, whole, fetched, sem) = refs[:PARTS], refs[PARTS:-5], refs[-5:]
    rows = NODES // PARTS
    half = rows // 2
    copy = pltpu.make_async_copy(bands[0], fetched, sem)
    copy.start()
    for k, piece in enumerate(pieces):
        whole[k * rows:(k + 1) * rows, :] = piece[...]
    for dx in (1, 2, 3, 0):
        if dx == 0:
            copy.wait()
        band = bands[dx] if dx else fetched
        total = jnp.dot(band[...], whole[...], preferred_element_type=jnp.float32)
        keep_ref[dx * half:(dx + 1) * half, :] = total[:half].astype(keep_ref.dtype)
        send_ref[dx * half:(dx + 1) * half, :] = total[half:].astype(send_ref.dtype)


def banded_call(kernel, name, outs, bands, in_hbm, fetched, pieces, after, limit):
    vmem = pl.BlockSpec(memory_space=pltpu.VMEM)
    spaces = [pltpu.HBM if k < in_hbm else pltpu.VMEM for k in range(len(bands))]
    return pl.pallas_call(
        kernel,
        in_specs=[pl.BlockSpec(memory_space=pl.ANY)] + [pl.BlockSpec(memory_space=m) for m in spaces]
        + [vmem] * len(pieces),
        out_specs=[vmem] * len(outs),
        out_shape=outs,
        scratch_shapes=[pltpu.VMEM((NODES, F), jnp.bfloat16)] + fetched,
        compiler_params=pltpu.CompilerParams(vmem_limit_bytes=limit * 1024 * 1024),
        cost_estimate=pl.CostEstimate(flops=0, bytes_accessed=0, transcendentals=0),
        name=name,
    )(after, *[pltpu.with_memory_space_constraint(b, m) for b, m in zip(bands, spaces)], *pieces)


def forward_part(bands, pieces, after):
    out = jax.ShapeDtypeStruct((NODES // 2, F), jnp.bfloat16)
    fetched = [pltpu.VMEM((NODES // PARTS, NODES), jnp.bfloat16), pltpu.SemaphoreType.DMA]
    return banded_call(forward_kernel, "forward_part", [out, out], bands, 1, fetched, pieces, after, 13)


def backward_kernel(dy, after_ref, *refs):
    bands, pieces, (out_ref, whole, fetched, sem) = refs[:PARTS], refs[PARTS:-4], refs[-4:]
    rows = NODES // 4
    columns = slice(dy * rows, (dy + 1) * rows)
    copy = pltpu.make_async_copy(bands[0].at[:, pl.ds(dy * rows, rows)], fetched, sem)
    copy.start()
    for k, piece in enumerate(pieces):
        size = piece.shape[0]
        whole[k * size:(k + 1) * size, :] = piece[...]
    copy.wait()
    dense = jnp.concatenate([fetched[...]] + [band[:, columns] for band in bands[1:]], 0)
    total = lax.dot_general(dense, whole[...], (((0,), (0,)), ((), ())), preferred_element_type=jnp.float32)
    out_ref[...] = total.astype(out_ref.dtype)


def backward_part(bands, pieces, dy, after):
    out = jax.ShapeDtypeStruct((NODES // 4, F), jnp.bfloat16)
    fetched = [pltpu.VMEM((NODES // PARTS, NODES // 4), jnp.bfloat16), pltpu.SemaphoreType.DMA]
    return banded_call(
        functools.partial(backward_kernel, dy), "backward_part", [out], bands, 1, fetched, pieces, after, 6)[0]


def rows_shift(dz, dy):
    return [(z * 4 + y, (z + dz) % 4 * 4 + (y + dy) % 4) for z in range(4) for y in range(4)]


def cols_shift(dz, dx, dc):
    return [
        (z * 8 + x * 2 + c, (z + dz) % 2 * 8 + (x + dx) % 4 * 2 + (c + dc) % 2)
        for z in range(2) for x in range(4) for c in range(2)
    ]


def f32(x):
    return x.astype(jnp.float32)


def bf16(x):
    return x.astype(jnp.bfloat16)


def dot(a, b, ca=1, cb=0):
    return lax.dot_general(a, b, (((ca,), (cb,)), ((), ())), preferred_element_type=jnp.float32)


def mix():
    nodes = lax.broadcasted_iota(jnp.int32, (256, 256), 0)
    natural = lax.broadcasted_iota(jnp.int32, (256, 256), 1)
    inner = nodes & (TB - 1)
    source = (nodes & ~(TB - 1)) + (inner & (PAIRS - 1)) * 2 + (inner >> 5)
    return bf16(source == natural)


def body(features, weight, tile_values, tile_rows, tile_cols, tile_count, out_grad):
    me_r = lax.axis_index("rows")
    me_c = lax.axis_index("cols")
    own = tile_rows[0, 0] >> 2
    slot_r = (((own >> 1) - (me_c >> 1)) & 3) * 4 + ((own ^ me_c) & 1) * 2 + (((own ^ me_c) >> 3) & 1)
    rows = slot_r * 4 + (tile_rows[0, 0] & 3)
    own = tile_cols[0, 0] >> 2
    slot_c = ((own - me_r) & 3) * 4 + (((own >> 2) - (me_r >> 2)) & 3)
    cols = slot_c * 4 + (tile_cols[0, 0] & 3)

    with jax.named_scope("gather_features"):
        block = jnp.concatenate(
            [features] + [lax.ppermute(features, "rows", rows_shift(-dz, 0)) for dz in (1, 2, 3)], 0)
        grad = lax.ppermute(out_grad, "cols", cols_shift(1, 0, 0))
        order, ends = plan_tiles(rows, cols, tile_count[0, 0])
        where = tuple((me_c >> 1 & 3) == x for x in (1, 2, 3)) + ((me_c & 1) == 0, (me_c >> 3) == 0)
        block, grad, order, ends, where = lax.optimization_barrier((block, grad, order, ends, where))
        sources = [block] + [lax.ppermute(block, "rows", rows_shift(0, -dy)) for dy in (1, 2, 3)]
    with jax.named_scope("build"):
        bands = build_dense(tile_values[0, 0], cols, order, ends, block)
    with jax.named_scope("forward"):
        keep, send = forward_part(bands, sources, block)
    with jax.named_scope("reduce_cols"):
        part = f32(keep) + f32(lax.ppermute(send, "cols", cols_shift(0, 0, 1)))
        sent = bf16(part[512:])
        part = part[:512]
        for dx in (2, 1, 3):
            part = part + f32(lax.ppermute(sent[512 * (dx - 1):512 * dx], "cols", cols_shift(0, dx, 0)))
        got = f32(lax.ppermute(bf16(part), "cols", cols_shift(1, 0, 0)))
        gathered = part + jnp.concatenate([got[256:], got[:256]], 0)
        high = bf16(gathered)
        low = bf16(gathered - f32(high))
        summed = dot(high, weight) + dot(low, weight)
    with jax.named_scope("activate"):
        turn = mix()
        grad = jnp.concatenate([dot(turn, out_grad), dot(turn, grad)], 0)
        sig = jax.nn.sigmoid(summed)
        block = bf16(grad * sig * (1.0 + summed * (1.0 - sig)))
        hidden = bf16(dot(turn, bf16(summed[:256] * sig[:256]), 0, 0))
    with jax.named_scope("gather_slope"):
        slopes = []
        for dx in range(4):
            mine = lax.ppermute(block, "cols", cols_shift(0, -dx, 0)) if dx else block
            slopes += [mine, lax.ppermute(mine, "cols", cols_shift(0, 0, 1))]
    with jax.named_scope("weight_grad"):
        half = jnp.where(where[4], block[:, :128], block[:, 128:])
        share = dot(half, high, 0, 0) + dot(half, low, 0, 0)
        turned = share
        for x in (1, 2, 3):
            turned = jnp.where(where[x - 1], jnp.concatenate([share[32 * x:], share[:32 * x]], 0), turned)
        band = turned[:32]
        for dx in (1, 2, 3):
            band = band + lax.ppermute(turned[32 * dx:32 * (dx + 1)], "cols", cols_shift(0, dx, 0))
        mine = jnp.where(where[3], band[:16], band[16:])
        other = jnp.where(where[3], band[16:], band[:16])
        band = mine + lax.ppermute(other, "cols", cols_shift(0, 0, 1))
    got = {}
    for dy in (2, 1, 3, 0):
        with jax.named_scope("backward"):
            terms = backward_part(bands, slopes, dy, slopes[0])
        with jax.named_scope("reduce_rows"):
            got[dy] = f32(lax.ppermute(terms, "rows", rows_shift(0, dy)) if dy else terms)
    band, got[0] = lax.optimization_barrier((band, got[0]))
    with jax.named_scope("reduce_rows"):
        part = got[0] + got[1] + got[2] + got[3]
        sent = bf16(part[256:])
        got = [lax.ppermute(sent[256 * (d - 1):256 * d], "rows", rows_shift(d, 0)) for d in (1, 2, 3)]
        back = bf16(part[:256] + f32(got[0]) + f32(got[1]) + f32(got[2]))
    with jax.named_scope("feature_grad"):
        feature_grad = bf16(dot(back, weight, 1, 1))
    with jax.named_scope("weight_grad"):
        band = band.reshape(16, 16, 16).transpose(1, 0, 2).reshape(16, 256)
        band = lax.all_to_all(band, "rows", 0, 0, tiled=True)
        weight_grad = jnp.sum(band, axis=0).reshape(16, 16).T
    return hidden, feature_grad, weight_grad


def solution(mesh):
    return jax.shard_map(
        body,
        mesh=mesh,
        in_specs=(
            P(("cols", "rows"), None),
            P(),
            P("rows", "cols", None, None),
            P("rows", "cols", None),
            P("rows", "cols", None),
            P("rows", "cols"),
            P(("rows", "cols"), None),
        ),
        out_specs=(P(("rows", "cols"), None), P(("cols", "rows"), None), P("rows", "cols")),
        check_vma=False,
    )
```

```python
import functools
import jax
import jax.numpy as jnp
from jax import lax
from jax.experimental import pallas as pl
from jax.experimental.pallas import tpu as pltpu
from jax.sharding import PartitionSpec as P

TB = 64
PAIRS = TB // 2
GROUP = 16
SIDE = 64
TILES = 768
WIDE = SIDE // 2
F = 256
BANDS = (0, 512, 1024, 2048, 3072, 4096)
PARTS = len(BANDS) - 1
UNROLL = 8
NODES = SIDE * TB
SLAB = 64


def plan_tiles(rows, cols, count):
    index = jnp.arange(TILES, dtype=jnp.int32)
    live = index < count
    pair = rows * WIDE + (cols >> 1)
    key = jnp.where(live, pair, SIDE * WIDE) * 1024 + index
    rank = jnp.sum((key[None, :] < key[:, None]).astype(jnp.int32), axis=1)
    code = index + 1024 * pair
    order = jnp.sum(jnp.where(rank[None, :] == index[:, None], code[None, :], 0), axis=1)
    ends = jnp.stack([jnp.sum((live & (rows < edge // TB)).astype(jnp.int32)) for edge in BANDS[1:]])
    return order, ends


def build_kernel(order_ref, ends_ref, cols_ref, vals_ref, after_ref, *refs):
    out_ref, *parts = refs[:PARTS]
    staged, vals, turned_ref, lay, sems = refs[PARTS:]
    parts = [staged, *parts]
    slabs = TILES // SLAB
    lane_half = lax.broadcasted_iota(jnp.int32, (PAIRS, 128), 1) >> 6

    def fetch(i):
        return pltpu.make_async_copy(vals_ref.at[pl.ds(i * SLAB, SLAB)], vals.at[i & 1], sems.at[i & 1])

    fetch(0).start()

    def clear(i, carry):
        for ref in parts:
            step = max(ref.shape[0] // SIDE, 16)
            turn = i if step * SIDE == ref.shape[0] else i >> 1
            ref[pl.ds(pl.multiple_of(turn * step, step), step), :] = jnp.zeros((step, NODES), ref.dtype)
        return carry

    def relay_slab(i, carry):
        @pl.when(i + 1 < slabs)
        def _():
            fetch(i + 1).start()

        lax.fori_loop(i * (SIDE // slabs), (i + 1) * (SIDE // slabs), clear, 0)
        fetch(i).wait()

        def relay(g, carry):
            for m in range(PAIRS):
                lay[m * GROUP:(m + 1) * GROUP, :] = vals[
                    i & 1, pl.ds(pl.multiple_of(g * GROUP, GROUP), GROUP), m * 128:(m + 1) * 128
                ].astype(jnp.float32)
            base = i * SLAB + g * GROUP
            for k in range(GROUP):
                turned_ref[base + k] = lay[pl.ds(k, PAIRS, stride=GROUP), :].astype(turned_ref.dtype)
            return carry

        lax.fori_loop(0, SLAB // GROUP, relay, 0)
        return carry

    lax.fori_loop(0, slabs, relay_slab, 0)
    lax.fori_loop(slabs * (SIDE // slabs), SIDE, clear, 0)
    none = jnp.zeros((PAIRS, 128), jnp.float32)
    for part, dense_ref in enumerate(parts):
        begin = ends_ref[part - 1] if part else 0
        end = ends_ref[part]

        def put(i, carry):
            before, even, odd = carry
            for k in range(UNROLL):
                spot = begin + i * UNROLL + k
                code = order_ref[jnp.minimum(spot, end - 1)]
                place = (code >> 10) - BANDS[part] // TB * WIDE
                keep = jnp.where(place == before, 1.0, 0.0)
                right = cols_ref[code & 1023] & 1
                tile = turned_ref[code & 1023].astype(jnp.float32)
                other = pltpu.roll(tile, TB, 1)
                mine = lane_half == jnp.where(spot < end, right, 2)
                left = right == 0
                even = even * keep + jnp.where(mine, jnp.where(left, tile, other), 0.0)
                odd = odd * keep + jnp.where(mine, jnp.where(left, other, tile), 0.0)
                before = place
                top = pl.multiple_of((place >> 5) << 6, TB)
                lanes = pl.ds(pl.multiple_of((place & 31) << 7, 128), 128)
                dense_ref[pl.ds(top, PAIRS), lanes] = even.astype(dense_ref.dtype)
                dense_ref[pl.ds(top + PAIRS, PAIRS), lanes] = odd.astype(dense_ref.dtype)
            return before, even, odd

        lax.fori_loop(0, (end - begin + UNROLL - 1) >> 3, put, (jnp.int32(-1), none, none))
        if part == 0:
            store = pltpu.make_async_copy(staged, out_ref, sems.at[2])
            store.start()
    store.wait()


def build_dense(values, cols, order, ends, after):
    smem = pl.BlockSpec(memory_space=pltpu.SMEM)
    anywhere = pl.BlockSpec(memory_space=pl.ANY)
    return pl.pallas_call(
        build_kernel,
        in_specs=[smem, smem, smem, pl.BlockSpec(memory_space=pltpu.HBM), anywhere],
        out_specs=[pl.BlockSpec(memory_space=pltpu.HBM)] + [pl.BlockSpec(memory_space=pltpu.VMEM)] * (PARTS - 1),
        out_shape=[pltpu.HBM((BANDS[1], NODES), jnp.bfloat16)]
        + [pltpu.VMEM((b - a, NODES), jnp.bfloat16) for a, b in zip(BANDS[1:], BANDS[2:])],
        scratch_shapes=[
            pltpu.VMEM((BANDS[1], NODES), jnp.bfloat16),
            pltpu.VMEM((2, SLAB, TB * TB), jnp.bfloat16),
            pltpu.VMEM((TILES, PAIRS, 128), jnp.bfloat16),
            pltpu.VMEM((GROUP * PAIRS, 128), jnp.float32),
            pltpu.SemaphoreType.DMA((3,)),
        ],
        compiler_params=pltpu.CompilerParams(vmem_limit_bytes=14 * 1024 * 1024),
        cost_estimate=pl.CostEstimate(flops=0, bytes_accessed=0, transcendentals=0),
        name="build_dense",
    )(order, ends, cols, pltpu.with_memory_space_constraint(values, pltpu.HBM), after)


def forward_kernel(after_ref, *refs):
    bands, pieces, (keep_ref, send_ref, whole, fetched, sem) = refs[:PARTS], refs[PARTS:-5], refs[-5:]
    rows = NODES // 4
    half = rows // 2
    copy = pltpu.make_async_copy(bands[0], fetched, sem)
    copy.start()
    for k, piece in enumerate(pieces):
        whole[k * rows:(k + 1) * rows, :] = piece[...]
    for part in (*range(1, PARTS), 0):
        if part == 0:
            copy.wait()
        band = bands[part] if part else fetched
        total = jnp.dot(band[...], whole[...], preferred_element_type=jnp.float32)
        for top in range(BANDS[part], BANDS[part + 1], half):
            dx, core = top // rows, top % rows // half
            out = send_ref if core else keep_ref
            begin = top - BANDS[part]
            out[dx * half:(dx + 1) * half, :] = total[begin:begin + half].astype(out.dtype)


def banded_call(kernel, name, outs, bands, in_hbm, fetched, pieces, after, limit):
    vmem = pl.BlockSpec(memory_space=pltpu.VMEM)
    spaces = [pltpu.HBM if k < in_hbm else pltpu.VMEM for k in range(len(bands))]
    return pl.pallas_call(
        kernel,
        in_specs=[pl.BlockSpec(memory_space=pl.ANY)] + [pl.BlockSpec(memory_space=m) for m in spaces]
        + [vmem] * len(pieces),
        out_specs=[vmem] * len(outs),
        out_shape=outs,
        scratch_shapes=[pltpu.VMEM((NODES, F), jnp.bfloat16)] + fetched,
        compiler_params=pltpu.CompilerParams(vmem_limit_bytes=limit * 1024 * 1024),
        cost_estimate=pl.CostEstimate(flops=0, bytes_accessed=0, transcendentals=0),
        name=name,
    )(after, *[pltpu.with_memory_space_constraint(b, m) for b, m in zip(bands, spaces)], *pieces)


def forward_part(bands, pieces, after):
    out = jax.ShapeDtypeStruct((NODES // 2, F), jnp.bfloat16)
    fetched = [pltpu.VMEM((BANDS[1], NODES), jnp.bfloat16), pltpu.SemaphoreType.DMA]
    return banded_call(forward_kernel, "forward_part", [out, out], bands, 1, fetched, pieces, after, 8)


def backward_kernel(dy, after_ref, *refs):
    bands, pieces, (out_ref, whole, fetched, sem) = refs[:PARTS], refs[PARTS:-4], refs[-4:]
    rows = NODES // 4
    columns = slice(dy * rows, (dy + 1) * rows)
    copy = pltpu.make_async_copy(bands[0].at[:, pl.ds(dy * rows, rows)], fetched, sem)
    copy.start()
    for k, piece in enumerate(pieces):
        size = piece.shape[0]
        whole[k * size:(k + 1) * size, :] = piece[...]
    copy.wait()
    dense = jnp.concatenate([fetched[...]] + [band[:, columns] for band in bands[1:]], 0)
    total = lax.dot_general(dense, whole[...], (((0,), (0,)), ((), ())), preferred_element_type=jnp.float32)
    out_ref[...] = total.astype(out_ref.dtype)


def backward_part(bands, pieces, dy, after):
    out = jax.ShapeDtypeStruct((NODES // 4, F), jnp.bfloat16)
    fetched = [pltpu.VMEM((BANDS[1], NODES // 4), jnp.bfloat16), pltpu.SemaphoreType.DMA]
    return banded_call(
        functools.partial(backward_kernel, dy), "backward_part", [out], bands, 1, fetched, pieces, after, 6)[0]


def rows_shift(dz, dy):
    return [(z * 4 + y, (z + dz) % 4 * 4 + (y + dy) % 4) for z in range(4) for y in range(4)]


def cols_shift(dz, dx, dc):
    return [
        (z * 8 + x * 2 + c, (z + dz) % 2 * 8 + (x + dx) % 4 * 2 + (c + dc) % 2)
        for z in range(2) for x in range(4) for c in range(2)
    ]


def f32(x):
    return x.astype(jnp.float32)


def bf16(x):
    return x.astype(jnp.bfloat16)


def dot(a, b, ca=1, cb=0):
    return lax.dot_general(a, b, (((ca,), (cb,)), ((), ())), preferred_element_type=jnp.float32)


def mix():
    nodes = lax.broadcasted_iota(jnp.int32, (256, 256), 0)
    natural = lax.broadcasted_iota(jnp.int32, (256, 256), 1)
    inner = nodes & (TB - 1)
    source = (nodes & ~(TB - 1)) + (inner & (PAIRS - 1)) * 2 + (inner >> 5)
    return bf16(source == natural)


def body(features, weight, tile_values, tile_rows, tile_cols, tile_count, out_grad):
    me_r = lax.axis_index("rows")
    me_c = lax.axis_index("cols")
    own = tile_rows[0, 0] >> 2
    slot_r = (((own >> 1) - (me_c >> 1)) & 3) * 4 + ((own ^ me_c) & 1) * 2 + (((own ^ me_c) >> 3) & 1)
    rows = slot_r * 4 + (tile_rows[0, 0] & 3)
    own = tile_cols[0, 0] >> 2
    slot_c = ((own - me_r) & 3) * 4 + (((own >> 2) - (me_r >> 2)) & 3)
    cols = slot_c * 4 + (tile_cols[0, 0] & 3)

    with jax.named_scope("gather_features"):
        block = jnp.concatenate(
            [features] + [lax.ppermute(features, "rows", rows_shift(-dz, 0)) for dz in (1, 2, 3)], 0)
        grad = lax.ppermute(out_grad, "cols", cols_shift(1, 0, 0))
        order, ends = plan_tiles(rows, cols, tile_count[0, 0])
        where = tuple((me_c >> 1 & 3) == x for x in (1, 2, 3)) + ((me_c & 1) == 0, (me_c >> 3) == 0)
        block, grad, order, ends, where = lax.optimization_barrier((block, grad, order, ends, where))
        sources = [block] + [lax.ppermute(block, "rows", rows_shift(0, -dy)) for dy in (1, 2, 3)]
    with jax.named_scope("build"):
        bands = build_dense(tile_values[0, 0], cols, order, ends, block)
    with jax.named_scope("forward"):
        keep, send = forward_part(bands, sources, block)
    with jax.named_scope("reduce_cols"):
        part = f32(keep) + f32(lax.ppermute(send, "cols", cols_shift(0, 0, 1)))
        sent = bf16(part[512:])
        part = part[:512]
        for dx in (2, 1, 3):
            part = part + f32(lax.ppermute(sent[512 * (dx - 1):512 * dx], "cols", cols_shift(0, dx, 0)))
        got = f32(lax.ppermute(bf16(part), "cols", cols_shift(1, 0, 0)))
        gathered = part + jnp.concatenate([got[256:], got[:256]], 0)
        high = bf16(gathered)
        low = bf16(gathered - f32(high))
        summed = dot(high, weight) + dot(low, weight)
    with jax.named_scope("activate"):
        turn = mix()
        grad = jnp.concatenate([dot(turn, out_grad), dot(turn, grad)], 0)
        sig = jax.nn.sigmoid(summed)
        block = bf16(grad * sig * (1.0 + summed * (1.0 - sig)))
        hidden = bf16(dot(turn, bf16(summed[:256] * sig[:256]), 0, 0))
    with jax.named_scope("gather_slope"):
        slopes = []
        for dx in range(4):
            mine = lax.ppermute(block, "cols", cols_shift(0, -dx, 0)) if dx else block
            slopes += [mine, lax.ppermute(mine, "cols", cols_shift(0, 0, 1))]
    with jax.named_scope("weight_grad"):
        half = jnp.where(where[4], block[:, :128], block[:, 128:])
        share = dot(half, high, 0, 0) + dot(half, low, 0, 0)
        turned = share
        for x in (1, 2, 3):
            turned = jnp.where(where[x - 1], jnp.concatenate([share[32 * x:], share[:32 * x]], 0), turned)
        band = turned[:32]
        for dx in (1, 2, 3):
            band = band + lax.ppermute(turned[32 * dx:32 * (dx + 1)], "cols", cols_shift(0, dx, 0))
        mine = jnp.where(where[3], band[:16], band[16:])
        other = jnp.where(where[3], band[16:], band[:16])
        band = mine + lax.ppermute(other, "cols", cols_shift(0, 0, 1))
    got = {}
    for dy in (2, 1, 3, 0):
        with jax.named_scope("backward"):
            terms = backward_part(bands, slopes, dy, slopes[0])
        with jax.named_scope("reduce_rows"):
            got[dy] = f32(lax.ppermute(terms, "rows", rows_shift(0, dy)) if dy else terms)
    band, got[0] = lax.optimization_barrier((band, got[0]))
    with jax.named_scope("reduce_rows"):
        part = got[0] + got[1] + got[2] + got[3]
        sent = bf16(part[256:])
        got = [lax.ppermute(sent[256 * (d - 1):256 * d], "rows", rows_shift(d, 0)) for d in (2, 1, 3)]
        back = bf16(part[:256] + f32(got[0]) + f32(got[1]) + f32(got[2]))
    with jax.named_scope("feature_grad"):
        feature_grad = bf16(dot(back, weight, 1, 1))
    with jax.named_scope("weight_grad"):
        band = band.reshape(16, 16, 16).transpose(1, 0, 2).reshape(16, 256)
        band = lax.all_to_all(band, "rows", 0, 0, tiled=True)
        weight_grad = jnp.sum(band, axis=0).reshape(16, 16).T
    return hidden, feature_grad, weight_grad


def solution(mesh):
    return jax.shard_map(
        body,
        mesh=mesh,
        in_specs=(
            P(("cols", "rows"), None),
            P(),
            P("rows", "cols", None, None),
            P("rows", "cols", None),
            P("rows", "cols", None),
            P("rows", "cols"),
            P(("rows", "cols"), None),
        ),
        out_specs=(P(("rows", "cols"), None), P(("cols", "rows"), None), P("rows", "cols")),
        check_vma=False,
    )
```

```python
import functools
import jax
import jax.numpy as jnp
from jax import lax
from jax.experimental import pallas as pl
from jax.experimental.pallas import tpu as pltpu
from jax.sharding import PartitionSpec as P

TB = 64
PAIRS = TB // 2
GROUP = 16
SIDE = 64
TILES = 768
WIDE = SIDE // 2
F = 256
BANDS = (0, 512, 1024, 2048, 3072, 4096)
PARTS = len(BANDS) - 1
UNROLL = 8
NODES = SIDE * TB
SLAB = 64


def plan_tiles(rows, cols, count):
    index = jnp.arange(TILES, dtype=jnp.int32)
    live = index < count
    pair = rows * WIDE + (cols >> 1)
    key = jnp.where(live, pair, SIDE * WIDE) * 1024 + index
    rank = jnp.sum((key[None, :] < key[:, None]).astype(jnp.int32), axis=1)
    code = index + 1024 * pair
    order = jnp.sum(jnp.where(rank[None, :] == index[:, None], code[None, :], 0), axis=1)
    ends = jnp.stack([jnp.sum((live & (rows < edge // TB)).astype(jnp.int32)) for edge in BANDS[1:]])
    return order, ends


def build_kernel(order_ref, ends_ref, cols_ref, vals_ref, after_ref, *refs):
    out_ref, *parts = refs[:PARTS]
    staged, vals, turned_ref, lay, sems = refs[PARTS:]
    parts = [staged, *parts]
    slabs = TILES // SLAB
    lane_half = lax.broadcasted_iota(jnp.int32, (PAIRS, 128), 1) >> 6

    def fetch(i):
        return pltpu.make_async_copy(vals_ref.at[pl.ds(i * SLAB, SLAB)], vals.at[i & 1], sems.at[i & 1])

    fetch(0).start()

    def clear(i, carry):
        for ref in parts:
            step = max(ref.shape[0] // SIDE, 16)
            turn = i if step * SIDE == ref.shape[0] else i >> 1
            ref[pl.ds(pl.multiple_of(turn * step, step), step), :] = jnp.zeros((step, NODES), ref.dtype)
        return carry

    def relay_slab(i, carry):
        @pl.when(i + 1 < slabs)
        def _():
            fetch(i + 1).start()

        lax.fori_loop(i * (SIDE // slabs), (i + 1) * (SIDE // slabs), clear, 0)
        fetch(i).wait()

        def relay(g, carry):
            for m in range(PAIRS):
                lay[m * GROUP:(m + 1) * GROUP, :] = vals[
                    i & 1, pl.ds(pl.multiple_of(g * GROUP, GROUP), GROUP), m * 128:(m + 1) * 128
                ].astype(jnp.float32)
            base = i * SLAB + g * GROUP
            for k in range(GROUP):
                turned_ref[base + k] = lay[pl.ds(k, PAIRS, stride=GROUP), :].astype(turned_ref.dtype)
            return carry

        lax.fori_loop(0, SLAB // GROUP, relay, 0)
        return carry

    lax.fori_loop(0, slabs, relay_slab, 0)
    lax.fori_loop(slabs * (SIDE // slabs), SIDE, clear, 0)
    none = jnp.zeros((PAIRS, 128), jnp.float32)
    for part, dense_ref in enumerate(parts):
        begin = ends_ref[part - 1] if part else 0
        end = ends_ref[part]

        def put(i, carry):
            before, even, odd = carry
            for k in range(UNROLL):
                spot = begin + i * UNROLL + k
                code = order_ref[jnp.minimum(spot, end - 1)]
                place = (code >> 10) - BANDS[part] // TB * WIDE
                keep = jnp.where(place == before, 1.0, 0.0)
                right = cols_ref[code & 1023] & 1
                tile = turned_ref[code & 1023].astype(jnp.float32)
                other = pltpu.roll(tile, TB, 1)
                mine = lane_half == jnp.where(spot < end, right, 2)
                left = right == 0
                even = even * keep + jnp.where(mine, jnp.where(left, tile, other), 0.0)
                odd = odd * keep + jnp.where(mine, jnp.where(left, other, tile), 0.0)
                before = place
                top = pl.multiple_of((place >> 5) << 6, TB)
                lanes = pl.ds(pl.multiple_of((place & 31) << 7, 128), 128)
                dense_ref[pl.ds(top, PAIRS), lanes] = even.astype(dense_ref.dtype)
                dense_ref[pl.ds(top + PAIRS, PAIRS), lanes] = odd.astype(dense_ref.dtype)
            return before, even, odd

        lax.fori_loop(0, (end - begin + UNROLL - 1) >> 3, put, (jnp.int32(-1), none, none))
        if part == 0:
            store = pltpu.make_async_copy(staged, out_ref, sems.at[2])
            store.start()
    store.wait()


def build_dense(values, cols, order, ends, after):
    smem = pl.BlockSpec(memory_space=pltpu.SMEM)
    anywhere = pl.BlockSpec(memory_space=pl.ANY)
    return pl.pallas_call(
        build_kernel,
        in_specs=[smem, smem, smem, pl.BlockSpec(memory_space=pltpu.HBM), anywhere],
        out_specs=[pl.BlockSpec(memory_space=pltpu.HBM)] + [pl.BlockSpec(memory_space=pltpu.VMEM)] * (PARTS - 1),
        out_shape=[pltpu.HBM((BANDS[1], NODES), jnp.bfloat16)]
        + [pltpu.VMEM((b - a, NODES), jnp.bfloat16) for a, b in zip(BANDS[1:], BANDS[2:])],
        scratch_shapes=[
            pltpu.VMEM((BANDS[1], NODES), jnp.bfloat16),
            pltpu.VMEM((2, SLAB, TB * TB), jnp.bfloat16),
            pltpu.VMEM((TILES, PAIRS, 128), jnp.bfloat16),
            pltpu.VMEM((GROUP * PAIRS, 128), jnp.float32),
            pltpu.SemaphoreType.DMA((3,)),
        ],
        compiler_params=pltpu.CompilerParams(vmem_limit_bytes=14 * 1024 * 1024),
        cost_estimate=pl.CostEstimate(flops=0, bytes_accessed=0, transcendentals=0),
        name="build_dense",
    )(order, ends, cols, pltpu.with_memory_space_constraint(values, pltpu.HBM), after)


def forward_kernel(after_ref, *refs):
    bands, pieces, (keep_ref, send_ref, whole, fetched, sem) = refs[:PARTS], refs[PARTS:-5], refs[-5:]
    rows = NODES // 4
    half = rows // 2
    copy = pltpu.make_async_copy(bands[0], fetched, sem)
    copy.start()
    for k, piece in enumerate(pieces):
        whole[k * rows:(k + 1) * rows, :] = piece[...]
    for part in (*range(1, PARTS), 0):
        if part == 0:
            copy.wait()
        band = bands[part] if part else fetched
        total = jnp.dot(band[...], whole[...], preferred_element_type=jnp.float32)
        for top in range(BANDS[part], BANDS[part + 1], half):
            dx, core = top // rows, top % rows // half
            out = send_ref if core else keep_ref
            begin = top - BANDS[part]
            out[dx * half:(dx + 1) * half, :] = total[begin:begin + half].astype(out.dtype)


def banded_call(kernel, name, outs, bands, in_hbm, fetched, pieces, after, limit):
    vmem = pl.BlockSpec(memory_space=pltpu.VMEM)
    spaces = [pltpu.HBM if k < in_hbm else pltpu.VMEM for k in range(len(bands))]
    return pl.pallas_call(
        kernel,
        in_specs=[pl.BlockSpec(memory_space=pl.ANY)] + [pl.BlockSpec(memory_space=m) for m in spaces]
        + [vmem] * len(pieces),
        out_specs=[vmem] * len(outs),
        out_shape=outs,
        scratch_shapes=[pltpu.VMEM((NODES, F), jnp.bfloat16)] + fetched,
        compiler_params=pltpu.CompilerParams(vmem_limit_bytes=limit * 1024 * 1024),
        cost_estimate=pl.CostEstimate(flops=0, bytes_accessed=0, transcendentals=0),
        name=name,
    )(after, *[pltpu.with_memory_space_constraint(b, m) for b, m in zip(bands, spaces)], *pieces)


def forward_part(bands, pieces, after):
    out = jax.ShapeDtypeStruct((NODES // 2, F), jnp.bfloat16)
    fetched = [pltpu.VMEM((BANDS[1], NODES), jnp.bfloat16), pltpu.SemaphoreType.DMA]
    return banded_call(forward_kernel, "forward_part", [out, out], bands, 1, fetched, pieces, after, 8)


def backward_kernel(dy, after_ref, *refs):
    bands, pieces, (out_ref, whole, fetched, sem) = refs[:PARTS], refs[PARTS:-4], refs[-4:]
    rows = NODES // 4
    columns = slice(dy * rows, (dy + 1) * rows)
    copy = pltpu.make_async_copy(bands[0].at[:, pl.ds(dy * rows, rows)], fetched, sem)
    copy.start()
    for k, piece in enumerate(pieces):
        size = piece.shape[0]
        whole[k * size:(k + 1) * size, :] = piece[...]
    copy.wait()
    dense = jnp.concatenate([fetched[...]] + [band[:, columns] for band in bands[1:]], 0)
    total = lax.dot_general(dense, whole[...], (((0,), (0,)), ((), ())), preferred_element_type=jnp.float32)
    out_ref[...] = total.astype(out_ref.dtype)


def backward_part(bands, pieces, dy, after):
    out = jax.ShapeDtypeStruct((NODES // 4, F), jnp.bfloat16)
    fetched = [pltpu.VMEM((BANDS[1], NODES // 4), jnp.bfloat16), pltpu.SemaphoreType.DMA]
    return banded_call(
        functools.partial(backward_kernel, dy), "backward_part", [out], bands, 1, fetched, pieces, after, 6)[0]


def rows_shift(dz, dy):
    return [(z * 4 + y, (z + dz) % 4 * 4 + (y + dy) % 4) for z in range(4) for y in range(4)]


def cols_shift(dz, dx, dc):
    return [
        (z * 8 + x * 2 + c, (z + dz) % 2 * 8 + (x + dx) % 4 * 2 + (c + dc) % 2)
        for z in range(2) for x in range(4) for c in range(2)
    ]


def f32(x):
    return x.astype(jnp.float32)


def bf16(x):
    return x.astype(jnp.bfloat16)


def dot(a, b, ca=1, cb=0):
    return lax.dot_general(a, b, (((ca,), (cb,)), ((), ())), preferred_element_type=jnp.float32)


def mix():
    nodes = lax.broadcasted_iota(jnp.int32, (256, 256), 0)
    natural = lax.broadcasted_iota(jnp.int32, (256, 256), 1)
    inner = nodes & (TB - 1)
    source = (nodes & ~(TB - 1)) + (inner & (PAIRS - 1)) * 2 + (inner >> 5)
    return bf16(source == natural)


def body(features, weight, tile_values, tile_rows, tile_cols, tile_count, out_grad):
    me_r = lax.axis_index("rows")
    me_c = lax.axis_index("cols")
    own = tile_rows[0, 0] >> 2
    slot_r = (((own >> 1) - (me_c >> 1)) & 3) * 4 + ((own ^ me_c) & 1) * 2 + (((own ^ me_c) >> 3) & 1)
    rows = slot_r * 4 + (tile_rows[0, 0] & 3)
    own = tile_cols[0, 0] >> 2
    slot_c = ((own - me_r) & 3) * 4 + (((own >> 2) - (me_r >> 2)) & 3)
    cols = slot_c * 4 + (tile_cols[0, 0] & 3)

    with jax.named_scope("gather_features"):
        block = jnp.concatenate(
            [features] + [lax.ppermute(features, "rows", rows_shift(-dz, 0)) for dz in (1, 2, 3)], 0)
        grad = lax.ppermute(out_grad, "cols", cols_shift(1, 0, 0))
        order, ends = plan_tiles(rows, cols, tile_count[0, 0])
        where = tuple((me_c >> 1 & 3) == x for x in (1, 2, 3)) + ((me_c & 1) == 0, (me_c >> 3) == 0)
        block, order, ends, where = lax.optimization_barrier((block, order, ends, where))
        sources = [block] + [lax.ppermute(block, "rows", rows_shift(0, -dy)) for dy in (1, 2, 3)]
    with jax.named_scope("build"):
        bands = build_dense(tile_values[0, 0], cols, order, ends, block)
    with jax.named_scope("forward"):
        keep, send = forward_part(bands, sources, block)
    with jax.named_scope("reduce_cols"):
        part = f32(keep) + f32(lax.ppermute(send, "cols", cols_shift(0, 0, 1)))
        sent = bf16(part[512:])
        part = part[:512]
        for dx in (2, 1, 3):
            part = part + f32(lax.ppermute(sent[512 * (dx - 1):512 * dx], "cols", cols_shift(0, dx, 0)))
        got = f32(lax.ppermute(bf16(part), "cols", cols_shift(1, 0, 0)))
        gathered = part + jnp.concatenate([got[256:], got[:256]], 0)
        high = bf16(gathered)
        low = bf16(gathered - f32(high))
        summed = dot(high, weight) + dot(low, weight)
    with jax.named_scope("activate"):
        turn = mix()
        grad = jnp.concatenate([dot(turn, out_grad), dot(turn, grad)], 0)
        sig = jax.nn.sigmoid(summed)
        block = bf16(grad * sig * (1.0 + summed * (1.0 - sig)))
        hidden = bf16(dot(turn, bf16(summed[:256] * sig[:256]), 0, 0))
    with jax.named_scope("gather_slope"):
        slopes = []
        for dx in range(4):
            mine = lax.ppermute(block, "cols", cols_shift(0, -dx, 0)) if dx else block
            slopes += [mine, lax.ppermute(mine, "cols", cols_shift(0, 0, 1))]
    with jax.named_scope("weight_grad"):
        half = jnp.where(where[4], block[:, :128], block[:, 128:])
        share = dot(half, high, 0, 0) + dot(half, low, 0, 0)
        turned = share
        for x in (1, 2, 3):
            turned = jnp.where(where[x - 1], jnp.concatenate([share[32 * x:], share[:32 * x]], 0), turned)
        band = turned[:32]
        for dx in (1, 2, 3):
            band = band + lax.ppermute(turned[32 * dx:32 * (dx + 1)], "cols", cols_shift(0, dx, 0))
        mine = jnp.where(where[3], band[:16], band[16:])
        other = jnp.where(where[3], band[16:], band[:16])
        band = mine + lax.ppermute(other, "cols", cols_shift(0, 0, 1))
    got = {}
    for dy in (2, 1, 3, 0):
        with jax.named_scope("backward"):
            terms = backward_part(bands, slopes, dy, slopes[0])
        with jax.named_scope("reduce_rows"):
            got[dy] = f32(lax.ppermute(terms, "rows", rows_shift(0, dy)) if dy else terms)
    band, got[0] = lax.optimization_barrier((band, got[0]))
    with jax.named_scope("reduce_rows"):
        part = got[0] + got[1] + got[2] + got[3]
        sent = bf16(part[256:])
        got = [lax.ppermute(sent[256 * (d - 1):256 * d], "rows", rows_shift(d, 0)) for d in (2, 1, 3)]
        back = bf16(part[:256] + f32(got[0]) + f32(got[1]) + f32(got[2]))
    with jax.named_scope("feature_grad"):
        feature_grad = bf16(dot(back, weight, 1, 1))
    with jax.named_scope("weight_grad"):
        band = band.reshape(16, 16, 16).transpose(1, 0, 2).reshape(16, 256)
        band = lax.all_to_all(band, "rows", 0, 0, tiled=True)
        weight_grad = jnp.sum(band, axis=0).reshape(16, 16).T
    return hidden, feature_grad, weight_grad


def solution(mesh):
    return jax.shard_map(
        body,
        mesh=mesh,
        in_specs=(
            P(("cols", "rows"), None),
            P(),
            P("rows", "cols", None, None),
            P("rows", "cols", None),
            P("rows", "cols", None),
            P("rows", "cols"),
            P(("rows", "cols"), None),
        ),
        out_specs=(P(("rows", "cols"), None), P(("cols", "rows"), None), P("rows", "cols")),
        check_vma=False,
    )
```
